32 devices in a mesh: seq: 4 (over y, x), chan: 8 (over z, core).
Axes of the slice: x: 2, y: 2, z: 4, core: 2. Of those that a mesh axis runs over, the one named last changes fastest.
Arguments:
- x_rows: bfloat16 [4096, 8192], P('seq'), may hold values from -6 to 6
- norm_gain: float32 [8192], replicated, may hold values from 0.1 to 1.9
- in_weight: bfloat16 [8192, 3, 8192], P('seq', None, 'chan'), may hold values from -0.0625 to 0.0625
- feat_filter: float32 [3, 3, 8192], P(None, None, 'chan'), may hold values from -3 to 3
- inner_filter: float32 [7, 8192], P(None, 'chan'), may hold values from -2.5 to 2.5
- out_weight: bfloat16 [8192, 8192], P('seq', 'chan'), may hold values from -0.0625 to 0.0625
Outputs:
- mixer_output: bfloat16 [4096, 8192], P(('seq', 'chan'))
The draws below stay inside these ranges and needn't reach their ends.
All inputs are finite; a program needn't handle non-finite values.
Results may differ from the reference program's by a relative error of at most 0.0086.
Values may be sent and summed in bfloat16 or wider, within the bound.
No kernel may reach another device: no remote copies, remote signals or barrier semaphores. Data moves between devices by JAX's collectives and lax.ppermute only.
A program may use at most 192 MiB of HBM per device.

```python
import jax
import jax.numpy as jnp
from jax import lax

D = 8192
FEAT = 3
FILT = 7
TOKENS = 4096


def level_of(own_key, shape, pieces, low, top_value):
    def one(position, blocks):
        heights = jax.random.uniform(jax.random.fold_in(jax.random.fold_in(own_key, 6), position), (blocks,), jnp.float32, low / len(pieces), top_value / len(pieces))
        return jnp.repeat(jnp.exp(heights), shape[position] // blocks).reshape((-1,) + (1,) * (len(shape) - position - 1))

    level = one(*pieces[0])
    for cut in pieces[1:]:
        level = level * one(*cut)
    return level


def normal_values(rng, shape, scale, most, shards=(), kind=jnp.bfloat16):
    array = jax.random.normal(rng, shape, jnp.float32) * scale
    if len(shards) > 0:
        array = level_of(rng, shape, shards, -0.22, 0.18) * array
    return jnp.clip(array, min=-most, max=most).astype(kind)


def setup_inputs(seed: int = 0) -> dict:
    key_of = jax.random.split(jax.random.key(seed), 7)
    return {
        "x_rows": normal_values(key_of[0], (TOKENS, D), 1.0, 6.0, ((0, 4),)),
        "norm_gain": jnp.clip(1.0 + 0.18 * jax.random.normal(key_of[1], (D,), jnp.float32), 0.1, 1.9),
        "in_weight": normal_values(key_of[2], (D, 3, D), D ** -0.5, 0.0625, ((0, 4), (2, 8))),
        "feat_filter": normal_values(key_of[3], (FEAT, 3, D), 0.6, 3.0, ((2, 8),), jnp.float32),
        "inner_filter": normal_values(key_of[4], (FILT, D), 0.4, 2.5, ((1, 8),), jnp.float32),
        "out_weight": normal_values(key_of[5], (D, D), D ** -0.5, 0.0625, ((0, 4), (1, 8))),
    }


def short_mix(extended, feat_filter, inner_filter, length):
    feat_taps = feat_filter.shape[0]
    inner_taps = inner_filter.shape[0]
    extent = length + inner_taps - 1
    offset = extended.shape[0] - extent
    featured = feat_filter[0] * extended[offset:offset + extent]
    for back_step in range(1, feat_taps):
        featured = featured + feat_filter[back_step] * extended[offset - back_step:offset - back_step + extent]
    product = featured[:, 1] * featured[:, 2]
    filtered = inner_filter[0] * product[inner_taps - 1:]
    for back_step in range(1, inner_taps):
        filtered = filtered + inner_filter[back_step] * product[inner_taps - 1 - back_step:inner_taps - 1 - back_step + length]
    return (featured[inner_taps - 1:, 0] * filtered).astype(jnp.bfloat16)

def reference(x_rows, norm_gain, in_weight, feat_filter, inner_filter, out_weight):
    values = x_rows.astype(jnp.float32)
    squares = lax.optimization_barrier(jnp.mean(values * values, axis=1, keepdims=True))
    normed = (values * lax.rsqrt(squares + 1e-06) * norm_gain).astype(jnp.bfloat16)
    width = in_weight.shape[0]
    projected = jnp.dot(normed, in_weight.reshape(width, 3 * width), preferred_element_type=jnp.float32)
    projected = projected.astype(jnp.bfloat16).reshape(normed.shape[0], 3, width)
    padding = jnp.zeros((FEAT + FILT - 2, 3, width), jnp.float32)
    extended = jnp.concatenate([padding, projected.astype(jnp.float32)], axis=0)
    gated_values = short_mix(extended, feat_filter, inner_filter, normed.shape[0])
    return jnp.dot(gated_values, out_weight, preferred_element_type=jnp.float32).astype(jnp.bfloat16)
```

```python
import functools

import jax
import jax.numpy as jnp
from jax import lax
from jax.experimental import pallas as pl
from jax.experimental.pallas import tpu as pltpu
from jax.sharding import PartitionSpec as P

HALO = 16
CHUNKS = 4
OUT_CHUNKS = 2
VMEM = 56 * 2**20


def project_kernel(count, extra, *refs):
    x_ref = refs[0]
    weights = refs[1 : 1 + count]
    received = refs[1 + count : 1 + count + extra]
    out_ref = refs[-1]
    depth = weights[0].shape[0]
    total = jnp.dot(x_ref[:, :depth], weights[0][...], preferred_element_type=jnp.float32)
    for i in range(1, count):
        total += jnp.dot(
            x_ref[:, i * depth : (i + 1) * depth],
            weights[i][...],
            preferred_element_type=jnp.float32,
        )
    for ref in received:
        total += ref[...].astype(jnp.float32)
    out_ref[...] = total.astype(out_ref.dtype)


def project(x, weights, received=()):
    rows, depth = x.shape
    columns = weights[0].shape[1]
    tile = min(rows, 256)
    whole = pl.BlockSpec(weights[0].shape, lambda i: (0, 0), pipeline_mode=pl.Buffered(1))
    return pl.pallas_call(
        functools.partial(project_kernel, len(weights), len(received)),
        grid=(rows // tile,),
        in_specs=[pl.BlockSpec((tile, depth), lambda i: (i, 0))]
        + [whole] * len(weights)
        + [pl.BlockSpec((tile, columns), lambda i: (i, 0))] * len(received),
        out_specs=pl.BlockSpec((tile, columns), lambda i: (i, 0)),
        out_shape=jax.ShapeDtypeStruct((rows, columns), jnp.bfloat16),
        compiler_params=pltpu.CompilerParams(vmem_limit_bytes=VMEM),
        cost_estimate=pl.CostEstimate(
            flops=2 * rows * depth * columns,
            bytes_accessed=2 * (rows * depth + depth * columns + (1 + len(received)) * rows * columns),
            transcendentals=0,
        ),
        name="project",
    )(x, *weights, *received)


def mix_kernel(feat, filt, qh, kh, vh, q, k, v, taps, out_ref, ext, prod):
    rows = q.shape[0]
    for i, (h, b) in enumerate(((qh, q), (kh, k), (vh, v))):
        ext[i, :HALO, :] = h[...].astype(jnp.float32)
        ext[i, HALO:, :] = b[...].astype(jnp.float32)
    tile = min(rows, 128)

    def featured(i, start, size):
        total = taps[i : i + 1, :] * ext[i, pl.ds(start, size), :]
        for j in range(1, feat):
            total += taps[3 * j + i : 3 * j + i + 1, :] * ext[i, pl.ds(start - j, size), :]
        return total

    for t in range(rows // tile):
        base = HALO + t * tile
        prod[...] = featured(1, base - 8, tile + 8) * featured(2, base - 8, tile + 8)
        total = taps[3 * feat : 3 * feat + 1, :] * prod[pl.ds(8, tile), :]
        for j in range(1, filt):
            total += taps[3 * feat + j : 3 * feat + j + 1, :] * prod[pl.ds(8 - j, tile), :]
        out_ref[t * tile : (t + 1) * tile, :] = (featured(0, base, tile) * total).astype(out_ref.dtype)


def short_mix(halo, projected, taps, feat, filt):
    rows, width = projected.shape[0], projected.shape[1] // 3
    lanes = 128
    steps = width // lanes

    def part(i, size):
        return pl.BlockSpec((size, lanes), lambda b: (0, i * steps + b))

    tile = min(rows, 128)
    return pl.pallas_call(
        functools.partial(mix_kernel, feat, filt),
        grid=(steps,),
        in_specs=[part(i, HALO) for i in range(3)]
        + [part(i, rows) for i in range(3)]
        + [pl.BlockSpec((taps.shape[0], lanes), lambda b: (0, b))],
        out_specs=pl.BlockSpec((rows, lanes), lambda b: (0, b)),
        out_shape=jax.ShapeDtypeStruct((rows, width), jnp.bfloat16),
        scratch_shapes=[
            pltpu.VMEM((3, HALO + rows, lanes), jnp.float32),
            pltpu.VMEM((tile + 8, lanes), jnp.float32),
        ],
        compiler_params=pltpu.CompilerParams(vmem_limit_bytes=VMEM),
        cost_estimate=pl.CostEstimate(
            flops=40 * rows * width, bytes_accessed=8 * rows * width, transcendentals=0
        ),
        name="short_mix",
    )(halo, halo, halo, projected, projected, projected, taps)


def out_kernel(blocks, parts, order, *refs):
    gated = refs[:parts]
    weights = refs[parts : parts + blocks]
    out_ref = refs[-1]
    width = gated[0].shape[2]
    per_block = weights[0].shape[0] // (width * parts)
    total = jnp.zeros(out_ref.shape, jnp.float32)
    for b in range(blocks):
        for i in range(per_block):
            for j in range(parts):
                row = (i * parts + j) * width
                total += jnp.dot(
                    gated[j][order[b] * per_block + i],
                    weights[b][row : row + width, :],
                    preferred_element_type=jnp.float32,
                )
    out_ref[...] = total.astype(out_ref.dtype)


def out_project(order, gated, weights):
    chans, rows, width = gated[0].shape
    depth, columns = weights[0].shape
    tile = min(rows, 256)
    spec = pltpu.PrefetchScalarGridSpec(
        num_scalar_prefetch=1,
        grid=(rows // tile,),
        in_specs=[pl.BlockSpec((chans, tile, width), lambda i, o: (0, i, 0))] * len(gated)
        + [pl.BlockSpec((depth, columns), lambda i, o: (0, 0), pipeline_mode=pl.Buffered(1))] * len(weights),
        out_specs=pl.BlockSpec((tile, columns), lambda i, o: (i, 0)),
    )
    total = depth * len(weights)
    return pl.pallas_call(
        functools.partial(out_kernel, len(weights), len(gated)),
        grid_spec=spec,
        out_shape=jax.ShapeDtypeStruct((rows, columns), jnp.bfloat16),
        compiler_params=pltpu.CompilerParams(vmem_limit_bytes=VMEM),
        cost_estimate=pl.CostEstimate(
            flops=2 * rows * total * columns,
            bytes_accessed=2 * (rows * total + total * columns + rows * columns),
            transcendentals=0,
        ),
        name="out_project",
    )(order, *gated, *weights)


def normalised(x, gain):
    values = x.astype(jnp.float32)
    squares = jnp.mean(values * values, axis=1, keepdims=True)
    return (values * lax.rsqrt(squares + 1e-06) * gain).astype(jnp.bfloat16)


def per_device(x_rows, norm_gain, in_weight, feat_filter, inner_filter, out_weight):
    tokens, model = x_rows.shape
    depth, _, chans_here = in_weight.shape
    seqs, chans = lax.axis_size("seq"), lax.axis_size("chan")
    near = 2 if seqs % 2 == 0 else 1
    far = seqs // near
    seq, chan = lax.axis_index("seq"), lax.axis_index("chan")
    e, g = seq // near, seq % near
    feat, filt = feat_filter.shape[0], inner_filter.shape[0]

    def from_near(block, k):
        pairs = [(a * near + (b + k) % near, a * near + b) for a in range(far) for b in range(near)]
        return lax.ppermute(block, "seq", pairs)

    def from_far(block, k):
        pairs = [((a + k) % far * near + b, a * near + b) for a in range(far) for b in range(near)]
        return lax.ppermute(block, "seq", pairs)

    def columns_of(rows, group):
        return jnp.concatenate(
            [
                lax.dynamic_slice_in_dim(rows, (group * near + (g + i) % near) * depth, depth, 1)
                for i in range(near)
            ],
            axis=1,
        )

    share = tokens // chans
    part = normalised(lax.dynamic_slice_in_dim(x_rows, chan * share, share, 0), norm_gain)
    theirs = []
    for k in range(1, far):
        piece = from_far(columns_of(part, (e - k) % far), k)
        full = lax.all_gather(piece, "chan", axis=0, tiled=True)
        theirs.append(full)
    mine = columns_of(normalised(x_rows, norm_gain), e)

    step = chans_here // CHUNKS
    taps = jnp.concatenate([feat_filter.reshape(feat * 3, chans_here), inner_filter], axis=0)
    gated = []
    for j in range(CHUNKS):
        cut = slice(j * step, (j + 1) * step)
        own = in_weight[:, :, cut].reshape(depth, 3 * step)
        weights = [own] + [from_near(own, k) for k in range(1, near)]
        sums = [
            from_far(project(theirs[k - 1], weights), far - k) for k in range(1, far)
        ]
        projected = project(mine, weights, sums)
        halo = lax.ppermute(
            projected[tokens - HALO :], "seq", [(i, i + 1) for i in range(seqs - 1)]
        )
        mixed = short_mix(halo, projected, taps[:, cut], feat, filt)
        gated.append(lax.all_gather(mixed, "chan", axis=0))

    order = jnp.stack(
        [(e + a) % far * near + (g + b) % near for a in range(far) for b in range(near)]
    ).astype(jnp.int32)
    width = out_weight.shape[1] // OUT_CHUNKS
    pieces = []
    for m in range(OUT_CHUNKS):
        own = out_weight[:, m * width : (m + 1) * width]
        row = [own] + [from_near(own, k) for k in range(1, near)]
        rows = row + [from_far(block, a) for a in range(1, far) for block in row]
        out = out_project(order, gated, rows)
        got = lax.all_to_all(
            out.reshape(chans, share, width), "chan", split_axis=0, concat_axis=0, tiled=True
        )
        pieces.append(got)
    return jnp.stack(pieces, axis=1).transpose(2, 0, 1, 3).reshape(share, -1)


def solution(mesh):
    return jax.shard_map(
        per_device,
        mesh=mesh,
        in_specs=(
            P("seq", None),
            P(),
            P("seq", None, "chan"),
            P(None, None, "chan"),
            P(None, "chan"),
            P("seq", "chan"),
        ),
        out_specs=P(("seq", "chan"), None),
        check_vma=False,
    )
```

```python
import functools

import jax
import jax.numpy as jnp
from jax import lax
from jax.experimental import pallas as pl
from jax.experimental.pallas import tpu as pltpu
from jax.sharding import PartitionSpec as P

HALO = 16
LANES = 128
EIGHTHS = (0, 2, 5, 7, 8)
CHUNKS = len(EIGHTHS) - 1
OUT_CHUNKS = 2
VMEM = 56 * 2**20
MARK = pl.BlockSpec((8, 128), lambda i: (0, 0))
MARK_SHAPE = jax.ShapeDtypeStruct((8, 128), jnp.float32)
LIGHT = pl.CostEstimate(flops=1024, bytes_accessed=1024, transcendentals=0)


def project_kernel(count, extra, *refs):
    x_ref = refs[0]
    weights = refs[1 : 1 + count]
    received = refs[1 + count : 1 + count + extra]
    out_ref, mark_ref = refs[-2:]
    mark_ref[...] = jnp.zeros_like(mark_ref)
    depth, width = weights[0].shape[1:]
    for part in range(weights[0].shape[0]):
        cut = slice(part * width, (part + 1) * width)
        total = jnp.dot(x_ref[:, :depth], weights[0][part], preferred_element_type=jnp.float32)
        for i in range(1, count):
            total += jnp.dot(
                x_ref[:, i * depth : (i + 1) * depth],
                weights[i][part],
                preferred_element_type=jnp.float32,
            )
        for ref in received:
            total += ref[:, cut].astype(jnp.float32)
        out_ref[:, cut] = total.astype(out_ref.dtype)


def project(x, weights, received=(), after=()):
    rows, depth = x.shape
    columns = weights[0].shape[0] * weights[0].shape[2]
    tile = min(rows, 256)
    whole = pl.BlockSpec(weights[0].shape, lambda i: (0, 0, 0), pipeline_mode=pl.Buffered(1))
    return pl.pallas_call(
        functools.partial(project_kernel, len(weights), len(received)),
        grid=(rows // tile,),
        in_specs=[pl.BlockSpec((tile, depth), lambda i: (i, 0))]
        + [whole] * len(weights)
        + [pl.BlockSpec((tile, columns), lambda i: (i, 0))] * len(received)
        + [pl.BlockSpec(memory_space=pl.ANY)] * len(after),
        out_specs=[pl.BlockSpec((tile, columns), lambda i: (i, 0)), MARK],
        out_shape=[jax.ShapeDtypeStruct((rows, columns), jnp.bfloat16), MARK_SHAPE],
        compiler_params=pltpu.CompilerParams(vmem_limit_bytes=VMEM),
        cost_estimate=LIGHT,
        name="project",
    )(x, *weights, *received, *after)


def mix_kernel(feat, filt, qh, kh, vh, q, k, v, taps, out_ref, mark_ref, ext, prod):
    rows = q.shape[0]
    mark_ref[...] = jnp.zeros_like(mark_ref)
    for i, (h, b) in enumerate(((qh, q), (kh, k), (vh, v))):
        ext[i, :HALO, :] = h[...].astype(jnp.float32)
        ext[i, HALO:, :] = b[...].astype(jnp.float32)
    tile = min(rows, 128)

    def featured(i, start, size):
        total = taps[i : i + 1, :] * ext[i, pl.ds(start, size), :]
        for j in range(1, feat):
            total += taps[3 * j + i : 3 * j + i + 1, :] * ext[i, pl.ds(start - j, size), :]
        return total

    for t in range(rows // tile):
        base = HALO + t * tile
        prod[...] = featured(1, base - 8, tile + 8) * featured(2, base - 8, tile + 8)
        total = taps[3 * feat : 3 * feat + 1, :] * prod[pl.ds(8, tile), :]
        for j in range(1, filt):
            total += taps[3 * feat + j : 3 * feat + j + 1, :] * prod[pl.ds(8 - j, tile), :]
        out_ref[t * tile : (t + 1) * tile, :] = (featured(0, base, tile) * total).astype(out_ref.dtype)


def short_mix(halo, projected, taps, feat, filt):
    rows, width = projected.shape[0], projected.shape[1] // 3
    lanes = LANES
    steps = width // lanes

    def part(i, size):
        return pl.BlockSpec((size, lanes), lambda b: (0, i * steps + b))

    tile = min(rows, 128)
    return pl.pallas_call(
        functools.partial(mix_kernel, feat, filt),
        grid=(steps,),
        in_specs=[part(i, HALO) for i in range(3)]
        + [part(i, rows) for i in range(3)]
        + [pl.BlockSpec((taps.shape[0], lanes), lambda b: (0, b))],
        out_specs=[pl.BlockSpec((rows, lanes), lambda b: (0, b)), MARK],
        out_shape=[jax.ShapeDtypeStruct((rows, width), jnp.bfloat16), MARK_SHAPE],
        scratch_shapes=[
            pltpu.VMEM((3, HALO + rows, lanes), jnp.float32),
            pltpu.VMEM((tile + 8, lanes), jnp.float32),
        ],
        compiler_params=pltpu.CompilerParams(vmem_limit_bytes=VMEM),
        cost_estimate=LIGHT,
        name="short_mix",
    )(halo, halo, halo, projected, projected, projected, taps)


def out_kernel(blocks, starts, order, *refs):
    gated = refs[: len(starts)]
    weights = refs[len(starts) : len(starts) + blocks]
    held, out_ref = refs[len(starts) + blocks : -1], refs[-1]
    depth = weights[0].shape[0]
    per_block = gated[0].shape[0] // blocks
    total = held[0][...] if held else jnp.zeros(out_ref.shape, jnp.float32)
    for b in range(blocks):
        for i in range(per_block):
            for ref, start in zip(gated, starts):
                row = i * (depth // per_block) + start
                total += jnp.dot(
                    ref[order[b] * per_block + i],
                    weights[b][row : row + ref.shape[2], :],
                    preferred_element_type=jnp.float32,
                )
    out_ref[...] = total.astype(out_ref.dtype)


def out_project(order, gated, starts, weights, kind, held=()):
    chans, rows, _ = gated[0].shape
    depth, columns = weights[0].shape
    tile, wide = min(rows, 256), min(columns, 512)
    cell = pl.BlockSpec((tile, wide), lambda n, i, o: (i, n))
    spec = pltpu.PrefetchScalarGridSpec(
        num_scalar_prefetch=1,
        grid=(columns // wide, rows // tile),
        in_specs=[pl.BlockSpec((chans, tile, block.shape[2]), lambda n, i, o: (0, i, 0)) for block in gated]
        + [pl.BlockSpec((depth, wide), lambda n, i, o: (0, n))] * len(weights)
        + [cell] * len(held),
        out_specs=cell,
    )
    return pl.pallas_call(
        functools.partial(out_kernel, len(weights), starts),
        grid_spec=spec,
        out_shape=jax.ShapeDtypeStruct((rows, columns), kind),
        compiler_params=pltpu.CompilerParams(vmem_limit_bytes=VMEM),
        cost_estimate=LIGHT,
        name="out_project",
    )(order, *gated, *weights, *held)


def normalised(x, gain):
    values = x.astype(jnp.float32)
    squares = jnp.mean(values * values, axis=1, keepdims=True)
    return (values * lax.rsqrt(squares + 1e-06) * gain).astype(jnp.bfloat16)


def per_device(x_rows, norm_gain, in_weight, feat_filter, inner_filter, out_weight):
    tokens, model = x_rows.shape
    depth, _, chans_here = in_weight.shape
    seqs, chans = lax.axis_size("seq"), lax.axis_size("chan")
    near = 2 if seqs % 2 == 0 else 1
    far = seqs // near
    seq, chan = lax.axis_index("seq"), lax.axis_index("chan")
    e, g = seq // near, seq % near
    feat, filt = feat_filter.shape[0], inner_filter.shape[0]

    def from_near(block, k):
        pairs = [(a * near + (b + k) % near, a * near + b) for a in range(far) for b in range(near)]
        return lax.ppermute(block, "seq", pairs)

    def from_far(block, k):
        pairs = [((a + k) % far * near + b, a * near + b) for a in range(far) for b in range(near)]
        return lax.ppermute(block, "seq", pairs)

    def columns_of(rows, group):
        return jnp.concatenate(
            [
                lax.dynamic_slice_in_dim(rows, (group * near + (g + i) % near) * depth, depth, 1)
                for i in range(near)
            ],
            axis=1,
        )

    together = lax.optimization_barrier
    units = chans_here // LANES
    edges = [LANES * (units * part // 8) for part in EIGHTHS]
    cuts = [slice(a, b) for a, b in zip(edges, edges[1:])]
    first = in_weight[:, :, cuts[0]].transpose(1, 0, 2)
    in_weight, first = together((in_weight, first))
    owns = [first] + [in_weight[:, :, cut].transpose(1, 0, 2) for cut in cuts[1:]]
    weights = [[own] + [from_near(own, k) for k in range(1, near)] for own in owns]
    width = out_weight.shape[1] // OUT_CHUNKS
    rows = [out_weight[:, m * width : (m + 1) * width] for m in range(OUT_CHUNKS)]

    share = tokens // chans
    part = normalised(lax.dynamic_slice_in_dim(x_rows, chan * share, share, 0), norm_gain)
    pieces = [
        from_far(columns_of(part, (e - k) % far), k) for k in range(1, far)
    ]
    pieces, rows, owns = together((pieces, rows, owns))
    theirs = [lax.all_gather(piece, "chan", axis=0, tiled=True) for piece in pieces]
    mine = columns_of(normalised(x_rows, norm_gain), e)
    taps = jnp.concatenate([feat_filter.reshape(feat * 3, chans_here), inner_filter], axis=0)

    across = [[from_far(block, a) for a in range(1, far)] for block in rows]
    theirs, weights[0], mine, across, rows = together(
        (theirs, weights[0], mine, across, rows)
    )
    near_rows = [[from_near(block, k) for k in range(1, near)] for block in rows]

    gated, done = [], []
    for j in range(CHUNKS):
        products = [project(block, weights[j], after=done)[0] for block in theirs]
        sums = [from_far(products[k - 1], far - k) for k in range(1, far)]
        if j < CHUNKS - 1:
            sums, weights[j + 1] = together((sums, weights[j + 1]))
        if j == CHUNKS - 1:
            sums, near_rows[0] = together((sums, near_rows[0]))
        projected, _ = project(mine, weights[j], sums)
        halo = lax.ppermute(
            projected[tokens - HALO :], "seq", [(a, a + 1) for a in range(seqs - 1)]
        )
        mixed, mark = short_mix(halo, projected, taps[:, cuts[j]], feat, filt)
        done = [mark]
        if j == CHUNKS - 1:
            mixed, near_rows = together((mixed, near_rows))
        if j > 0:
            mixed, gated[j - 1] = together((mixed, gated[j - 1]))
        gated.append(lax.all_gather(mixed, "chan", axis=0))

    order = jnp.stack(
        [(e + a) % far * near + (g + b) % near for a in range(far) for b in range(near)]
    ).astype(jnp.int32)
    sums = []
    blocks = []
    for m in range(OUT_CHUNKS):
        found = [rows[m]] + near_rows[m]
        for a in range(1, far):
            found += [across[m][a - 1]] + [from_far(block, a) for block in near_rows[m]]
        blocks.append(found)
        sums.append(out_project(order, gated[:-1], edges[: CHUNKS - 1], found, jnp.float32))
    sums, last = together((sums, gated[-1]))
    outs = [
        out_project(order, [last], [edges[CHUNKS - 1]], blocks[m], jnp.bfloat16, [sums[m]])
        for m in range(OUT_CHUNKS)
    ]
    out = jnp.concatenate(outs, axis=1).reshape(chans, share, -1)
    got = lax.all_to_all(out, "chan", split_axis=0, concat_axis=0, tiled=True)
    return got.transpose(1, 0, 2).reshape(share, -1)


def solution(mesh):
    return jax.shard_map(
        per_device,
        mesh=mesh,
        in_specs=(
            P("seq", None),
            P(),
            P("seq", None, "chan"),
            P(None, None, "chan"),
            P(None, "chan"),
            P("seq", "chan"),
        ),
        out_specs=P(("seq", "chan"), None),
        check_vma=False,
    )
```

```python
import functools

import jax
import jax.numpy as jnp
from jax import lax
from jax.experimental import pallas as pl
from jax.experimental.pallas import tpu as pltpu
from jax.sharding import PartitionSpec as P

HALO = 16
LANES = 128
EIGHTHS = (0, 2, 4, 6, 8)
CHUNKS = len(EIGHTHS) - 1
OUT_CHUNKS = 4
VMEM = 56 * 2**20
TILE = 512
MARK = pl.BlockSpec((8, 128), lambda i: (0, 0))
MARK_SHAPE = jax.ShapeDtypeStruct((8, 128), jnp.float32)
LIGHT = pl.CostEstimate(flops=1024, bytes_accessed=1024, transcendentals=0)


def project_kernel(count, extra, *refs):
    x_ref, halo_ref = refs[:2]
    weights = refs[2 : 2 + count]
    received = refs[2 + count : 2 + count + extra]
    received_halo = refs[2 + count + extra : 2 + count + 2 * extra]
    out_ref = refs[-1]
    parts, depth, width = weights[0].shape
    tile, halo = x_ref.shape[0], halo_ref.shape[0]
    step = pl.program_id(0)

    def products(ref, sums, start, size):
        for part in range(parts):
            cut = slice(part * width, (part + 1) * width)
            total = jnp.dot(ref[:, :depth], weights[0][part], preferred_element_type=jnp.float32)
            for i in range(1, count):
                total += jnp.dot(
                    ref[:, i * depth : (i + 1) * depth],
                    weights[i][part],
                    preferred_element_type=jnp.float32,
                )
            for other in sums:
                total += other[:, cut].astype(jnp.float32)
            out_ref[pl.ds(start, size), cut] = total.astype(out_ref.dtype)

    products(x_ref, received, pl.multiple_of(step * tile, tile), tile)

    @pl.when(step == 0)
    def _():
        products(halo_ref, received_halo, out_ref.shape[0] - halo, halo)


def project(x, halo, weights, received=(), after=()):
    rows, depth = x.shape
    extra = halo.shape[0]
    columns = weights[0].shape[0] * weights[0].shape[2]
    tile = min(rows, TILE)
    whole = pl.BlockSpec(weights[0].shape, lambda i: (0, 0, 0), pipeline_mode=pl.Buffered(1))
    return pl.pallas_call(
        functools.partial(project_kernel, len(weights), len(received)),
        grid=(rows // tile,),
        in_specs=[pl.BlockSpec((tile, depth), lambda i: (i, 0))]
        + [pl.BlockSpec((extra, depth), lambda i: (0, 0))]
        + [whole] * len(weights)
        + [pl.BlockSpec((tile, columns), lambda i: (i, 0))] * len(received)
        + [pl.BlockSpec((extra, columns), lambda i: (rows // extra, 0))] * len(received)
        + [pl.BlockSpec(memory_space=pl.ANY)] * len(after),
        out_specs=pl.BlockSpec((rows + extra, columns), lambda i: (0, 0)),
        out_shape=jax.ShapeDtypeStruct((rows + extra, columns), jnp.bfloat16),
        compiler_params=pltpu.CompilerParams(vmem_limit_bytes=VMEM),
        cost_estimate=LIGHT,
        name="project",
    )(x, halo, *weights, *received, *received, *after)


def mix_kernel(feat, filt, qh, kh, vh, q, k, v, taps, out_ref, mark_ref, ext, prod):
    rows = q.shape[0]
    mark_ref[...] = jnp.zeros_like(mark_ref)
    for i, (h, b) in enumerate(((qh, q), (kh, k), (vh, v))):
        ext[i, :HALO, :] = h[...].astype(jnp.float32)
        ext[i, HALO:, :] = b[...].astype(jnp.float32)
    tile = min(rows, 128)

    def featured(i, start, size):
        total = taps[i : i + 1, :] * ext[i, pl.ds(start, size), :]
        for j in range(1, feat):
            total += taps[3 * j + i : 3 * j + i + 1, :] * ext[i, pl.ds(start - j, size), :]
        return total

    for t in range(rows // tile):
        base = HALO + t * tile
        prod[...] = featured(1, base - 8, tile + 8) * featured(2, base - 8, tile + 8)
        total = taps[3 * feat : 3 * feat + 1, :] * prod[pl.ds(8, tile), :]
        for j in range(1, filt):
            total += taps[3 * feat + j : 3 * feat + j + 1, :] * prod[pl.ds(8 - j, tile), :]
        out_ref[t * tile : (t + 1) * tile, :] = (featured(0, base, tile) * total).astype(out_ref.dtype)


def short_mix(projected, taps, feat, filt):
    rows, width = projected.shape[0] - HALO, projected.shape[1] // 3
    lanes = LANES
    steps = width // lanes

    def part(i, size, row):
        return pl.BlockSpec((size, lanes), lambda b: (row, i * steps + b))

    tile = min(rows, 128)
    return pl.pallas_call(
        functools.partial(mix_kernel, feat, filt),
        grid=(steps,),
        in_specs=[part(i, HALO, rows // HALO) for i in range(3)]
        + [part(i, rows, 0) for i in range(3)]
        + [pl.BlockSpec((taps.shape[0], lanes), lambda b: (0, b))],
        out_specs=[pl.BlockSpec((rows, lanes), lambda b: (0, b)), MARK],
        out_shape=[jax.ShapeDtypeStruct((rows, width), jnp.bfloat16), MARK_SHAPE],
        scratch_shapes=[
            pltpu.VMEM((3, HALO + rows, lanes), jnp.float32),
            pltpu.VMEM((tile + 8, lanes), jnp.float32),
        ],
        compiler_params=pltpu.CompilerParams(vmem_limit_bytes=VMEM),
        cost_estimate=LIGHT,
        name="short_mix",
    )(*[projected] * 6, taps)


def out_kernel(blocks, count, columns, order, *refs):
    gated = refs[:count]
    weights = refs[count : count + blocks * columns]
    held, out_ref = refs[count + blocks * columns : -1], refs[-1]
    per_block, _, wide = weights[0].shape
    for m in range(columns):
        cut = slice(m * wide, (m + 1) * wide)
        total = held[0][:, cut] if held else jnp.zeros((out_ref.shape[0], wide), jnp.float32)
        for b in range(blocks):
            for i in range(per_block):
                row = 0
                for ref in gated:
                    size = ref.shape[2]
                    total += jnp.dot(
                        ref[order[b] * per_block + i],
                        weights[m * blocks + b][i, row : row + size, :],
                        preferred_element_type=jnp.float32,
                    )
                    row += size
        out_ref[:, cut] = total.astype(out_ref.dtype)


def out_project(order, gated, start, weights, kind, held=()):
    chans, rows, _ = gated[0].shape
    size = sum(block.shape[2] for block in gated)
    per_block, _, wide = weights[0][0].shape
    columns, blocks = len(weights), len(weights[0])
    tile = min(rows, 256)
    cell = pl.BlockSpec((tile, columns * wide), lambda i, o: (i, 0))
    piece = pl.BlockSpec(
        (per_block, size, wide), lambda i, o: (0, start // size, 0), pipeline_mode=pl.Buffered(1)
    )
    spec = pltpu.PrefetchScalarGridSpec(
        num_scalar_prefetch=1,
        grid=(rows // tile,),
        in_specs=[pl.BlockSpec((chans, tile, block.shape[2]), lambda i, o: (0, i, 0)) for block in gated]
        + [piece] * (columns * blocks)
        + [cell] * len(held),
        out_specs=cell,
    )
    return pl.pallas_call(
        functools.partial(out_kernel, blocks, len(gated), columns),
        grid_spec=spec,
        out_shape=jax.ShapeDtypeStruct((rows, columns * wide), kind),
        compiler_params=pltpu.CompilerParams(vmem_limit_bytes=VMEM),
        cost_estimate=LIGHT,
        name="out_project",
    )(order, *gated, *[block for found in weights for block in found], *held)


def normalised(x, gain):
    values = x.astype(jnp.float32)
    squares = jnp.mean(values * values, axis=1, keepdims=True)
    return (values * lax.rsqrt(squares + 1e-06) * gain).astype(jnp.bfloat16)


def per_device(x_rows, norm_gain, in_weight, feat_filter, inner_filter, out_weight):
    tokens, model = x_rows.shape
    depth, _, chans_here = in_weight.shape
    seqs, chans = lax.axis_size("seq"), lax.axis_size("chan")
    near = 2 if seqs % 2 == 0 else 1
    far = seqs // near
    seq, chan = lax.axis_index("seq"), lax.axis_index("chan")
    e, g = seq // near, seq % near
    feat, filt = feat_filter.shape[0], inner_filter.shape[0]

    def from_near(block, k):
        pairs = [(a * near + (b + k) % near, a * near + b) for a in range(far) for b in range(near)]
        return lax.ppermute(block, "seq", pairs)

    def from_far(block, k):
        pairs = [((a + k) % far * near + b, a * near + b) for a in range(far) for b in range(near)]
        return lax.ppermute(block, "seq", pairs)

    def columns_of(rows, group):
        return jnp.concatenate(
            [
                lax.dynamic_slice_in_dim(rows, (group * near + (g + i) % near) * depth, depth, 1)
                for i in range(near)
            ],
            axis=1,
        )

    together = lax.optimization_barrier
    units = chans_here // LANES
    edges = [LANES * (units * part // 8) for part in EIGHTHS]
    cuts = [slice(a, b) for a, b in zip(edges, edges[1:])]
    first = in_weight[:, :, cuts[0]].transpose(1, 0, 2)
    in_weight, first = together((in_weight, first))
    owns = [first] + [in_weight[:, :, cut].transpose(1, 0, 2) for cut in cuts[1:]]
    weights = [[own] + [from_near(own, k) for k in range(1, near)] for own in owns]
    width = out_weight.shape[1] // OUT_CHUNKS
    rows = [out_weight[:, m * width : (m + 1) * width] for m in range(OUT_CHUNKS)]

    near_rows = [[from_near(block, k) for k in range(1, near)] for block in rows]

    share = tokens // chans
    before = lax.ppermute(
        x_rows[tokens - HALO :], "seq", [(a, a + 1) for a in range(seqs - 1)]
    )
    part = normalised(lax.dynamic_slice_in_dim(x_rows, chan * share, share, 0), norm_gain)
    pieces = [
        from_far(columns_of(part, (e - k) % far), k) for k in range(1, far)
    ]
    pieces, rows, owns, near_rows[0] = together((pieces, rows, owns, near_rows[0]))
    theirs = [lax.all_gather(piece, "chan", axis=0, tiled=True) for piece in pieces]
    before = normalised(before, norm_gain)
    theirs_before = [from_far(columns_of(before, (e - k) % far), k) for k in range(1, far)]
    mine = columns_of(normalised(x_rows, norm_gain), e)
    mine_before = columns_of(before, e)
    taps = jnp.concatenate([feat_filter.reshape(feat * 3, chans_here), inner_filter], axis=0)

    across = [[from_far(block, a) for a in range(1, far)] for block in rows]
    theirs, theirs_before, weights[0], mine, mine_before, across = together(
        (theirs, theirs_before, weights[0], mine, mine_before, across)
    )

    gated, done = [], []
    for j in range(CHUNKS):
        sums = [
            from_far(project(theirs[k], theirs_before[k], weights[j], after=done), far - 1 - k)
            for k in range(far - 1)
        ]
        projected = project(mine, mine_before, weights[j], sums)
        if j == 0:
            projected, weights[1], near_rows[1] = together((projected, weights[1], near_rows[1]))
            beyond = [
                [from_far(block, a) for a in range(1, far) for block in found] for found in near_rows[:2]
            ]
        elif j < CHUNKS - 1:
            turn = min(j - 1, 1)
            projected, weights[j + 1], beyond[turn] = together(
                (projected, weights[j + 1], beyond[turn])
            )
        else:
            projected, near_rows[2:] = together((projected, near_rows[2:]))
            beyond += [
                [from_far(block, a) for a in range(1, far) for block in found] for found in near_rows[2:]
            ]
        mixed, mark = short_mix(projected, taps[:, cuts[j]], feat, filt)
        done = [mark]
        if j > 0:
            mixed, gated[j - 1] = together((mixed, gated[j - 1]))
        gated.append(lax.all_gather(mixed, "chan", axis=0))

    order = jnp.stack(
        [(e + a) % far * near + (g + b) % near for a in range(far) for b in range(near)]
    ).astype(jnp.int32)
    blocks = []
    for m in range(OUT_CHUNKS):
        found = [rows[m]] + near_rows[m]
        for a in range(1, far):
            found += [across[m][a - 1]] + beyond[m][(a - 1) * (near - 1) : a * (near - 1)]
        blocks.append([block.reshape(-1, chans_here, block.shape[1]) for block in found])
    half = OUT_CHUNKS // 2
    sums = [
        out_project(order, gated[:-1], 0, found, jnp.float32) for found in (blocks[:half], blocks[half:])
    ]
    sums, last = together((sums, gated[-1]))
    outs = [
        out_project(order, [last], edges[CHUNKS - 1], found, jnp.bfloat16, [total])
        for found, total in zip((blocks[:half], blocks[half:]), sums)
    ]
    out = jnp.concatenate(outs, axis=1).reshape(chans, share, -1)
    got = lax.all_to_all(out, "chan", split_axis=0, concat_axis=0, tiled=True)
    return got.transpose(1, 0, 2).reshape(share, -1)


def solution(mesh):
    return jax.shard_map(
        per_device,
        mesh=mesh,
        in_specs=(
            P("seq", None),
            P(),
            P("seq", None, "chan"),
            P(None, None, "chan"),
            P(None, "chan"),
            P("seq", "chan"),
        ),
        out_specs=P(("seq", "chan"), None),
        check_vma=False,
    )
```

```python
import functools

import jax
import jax.numpy as jnp
from jax import lax
from jax.experimental import pallas as pl
from jax.experimental.pallas import tpu as pltpu
from jax.sharding import PartitionSpec as P

HALO = 16
LANES = 128
EIGHTHS = (0, 2, 4, 6, 8)
CHUNKS = len(EIGHTHS) - 1
OUT_CHUNKS = 4
VMEM = 56 * 2**20
MARK = pl.BlockSpec((8, 128), lambda i: (0, 0))
MARK_SHAPE = jax.ShapeDtypeStruct((8, 128), jnp.float32)
LIGHT = pl.CostEstimate(flops=1024, bytes_accessed=1024, transcendentals=0)


def project_kernel(count, extra, *refs):
    x_ref, halo_ref = refs[:2]
    weights = refs[2 : 2 + count]
    received = refs[2 + count : 2 + count + extra]
    out_ref, total = refs[-2:]
    parts, _, width = weights[0].shape
    step, steps = pl.program_id(0), pl.num_programs(0)
    per_weight = steps // count
    lhs = jnp.concatenate([x_ref[...], halo_ref[...]], axis=0)
    for i, weight in enumerate(weights):

        @pl.when(step // per_weight == i)
        def _(weight=weight):
            for part in range(parts):
                cut = slice(part * width, (part + 1) * width)
                product = jnp.dot(lhs, weight[part], preferred_element_type=jnp.float32)

                @pl.when(step == 0)
                def _():
                    total[:, cut] = product

                @pl.when((step > 0) & (step < steps - 1))
                def _():
                    total[:, cut] += product

                @pl.when(step == steps - 1)
                def _():
                    value = total[:, cut] + product
                    for ref in received:
                        value += ref[:, cut].astype(jnp.float32)
                    out_ref[:, cut] = value.astype(out_ref.dtype)


def project(x, halo, weights, received=(), after=()):
    rows, depth = x.shape
    extra = halo.shape[0]
    parts, weight_depth, width = weights[0].shape
    columns = parts * width
    slab = weight_depth // 2
    steps = depth // slab

    def weight_spec(i):
        return pl.BlockSpec((parts, slab, width), lambda k: (0, jnp.clip(k - 2 * i, 0, 1), 0))

    result = pl.BlockSpec((rows + extra, columns), lambda k: (0, 0))
    return pl.pallas_call(
        functools.partial(project_kernel, len(weights), len(received)),
        grid=(steps,),
        in_specs=[pl.BlockSpec((rows, slab), lambda k: (0, k))]
        + [pl.BlockSpec((extra, slab), lambda k: (0, k))]
        + [weight_spec(i) for i in range(len(weights))]
        + [result] * len(received)
        + [pl.BlockSpec(memory_space=pl.ANY)] * len(after),
        out_specs=result,
        out_shape=jax.ShapeDtypeStruct((rows + extra, columns), jnp.bfloat16),
        scratch_shapes=[pltpu.VMEM((rows + extra, columns), jnp.float32)],
        compiler_params=pltpu.CompilerParams(vmem_limit_bytes=VMEM),
        cost_estimate=LIGHT,
        name="project",
    )(x, halo, *weights, *received, *after)


def mix_kernel(feat, filt, qh, kh, vh, q, k, v, taps, out_ref, mark_ref, ext, prod):
    rows = q.shape[0]
    mark_ref[...] = jnp.zeros_like(mark_ref)
    for i, (h, b) in enumerate(((qh, q), (kh, k), (vh, v))):
        ext[i, :HALO, :] = h[...].astype(jnp.float32)
        ext[i, HALO:, :] = b[...].astype(jnp.float32)
    tile = min(rows, 128)

    def featured(i, start, size):
        total = taps[i : i + 1, :] * ext[i, pl.ds(start, size), :]
        for j in range(1, feat):
            total += taps[3 * j + i : 3 * j + i + 1, :] * ext[i, pl.ds(start - j, size), :]
        return total

    for t in range(rows // tile):
        base = HALO + t * tile
        prod[...] = featured(1, base - 8, tile + 8) * featured(2, base - 8, tile + 8)
        total = taps[3 * feat : 3 * feat + 1, :] * prod[pl.ds(8, tile), :]
        for j in range(1, filt):
            total += taps[3 * feat + j : 3 * feat + j + 1, :] * prod[pl.ds(8 - j, tile), :]
        out_ref[t * tile : (t + 1) * tile, :] = (featured(0, base, tile) * total).astype(out_ref.dtype)


def short_mix(projected, taps, feat, filt):
    rows, width = projected.shape[0] - HALO, projected.shape[1] // 3
    lanes = LANES
    steps = width // lanes

    def part(i, size, row):
        return pl.BlockSpec((size, lanes), lambda b: (row, i * steps + b))

    tile = min(rows, 128)
    return pl.pallas_call(
        functools.partial(mix_kernel, feat, filt),
        grid=(steps,),
        in_specs=[part(i, HALO, rows // HALO) for i in range(3)]
        + [part(i, rows, 0) for i in range(3)]
        + [pl.BlockSpec((taps.shape[0], lanes), lambda b: (0, b))],
        out_specs=[pl.BlockSpec((rows, lanes), lambda b: (0, b)), MARK],
        out_shape=[jax.ShapeDtypeStruct((rows, width), jnp.bfloat16), MARK_SHAPE],
        scratch_shapes=[
            pltpu.VMEM((3, HALO + rows, lanes), jnp.float32),
            pltpu.VMEM((tile + 8, lanes), jnp.float32),
        ],
        compiler_params=pltpu.CompilerParams(vmem_limit_bytes=VMEM),
        cost_estimate=LIGHT,
        name="short_mix",
    )(*[projected] * 6, taps)


def out_kernel(blocks, columns, count, order, *refs):
    gated = refs[:count]
    weights = refs[count : count + columns * blocks]
    held, (out_ref, total) = refs[count + columns * blocks : -2], refs[-2:]
    per_block, _, wide = weights[0].shape
    step, steps = pl.program_id(0), pl.num_programs(0)
    lhs = jnp.concatenate([ref[0] for ref in gated], axis=1)
    for b in range(blocks):
        for i in range(per_block):

            @pl.when(step == b * per_block + i)
            def _(b=b, i=i):
                for m in range(columns):
                    cut = slice(m * wide, (m + 1) * wide)
                    value = jnp.dot(
                        lhs, weights[m * blocks + b][i], preferred_element_type=jnp.float32
                    )
                    if b + i > 0:
                        value += total[:, cut]
                    elif held:
                        each = columns // len(held)
                        value += held[m // each][:, m % each * wide : (m % each + 1) * wide]
                    if b == blocks - 1 and i == per_block - 1:
                        out_ref[:, cut] = value.astype(out_ref.dtype)
                    else:
                        total[:, cut] = value


def out_project(order, gated, start, weights, kind, held=()):
    chans, rows, _ = gated[0].shape
    size = sum(block.shape[2] for block in gated)
    per_block, _, wide = weights[0][0].shape
    columns, blocks = len(weights), len(weights[0])
    whole = [
        pl.BlockSpec(block.shape, lambda k, o: (0, 0), pipeline_mode=pl.Buffered(1)) for block in held
    ]
    piece = pl.BlockSpec(
        (per_block, size, wide), lambda k, o: (0, start // size, 0), pipeline_mode=pl.Buffered(1)
    )
    spec = pltpu.PrefetchScalarGridSpec(
        num_scalar_prefetch=1,
        grid=(chans,),
        in_specs=[
            pl.BlockSpec(
                (1, rows, block.shape[2]),
                lambda k, o: (o[k // per_block] * per_block + k % per_block, 0, 0),
            )
            for block in gated
        ]
        + [piece] * (columns * blocks)
        + whole,
        out_specs=pl.BlockSpec((rows, columns * wide), lambda k, o: (0, 0)),
        scratch_shapes=[pltpu.VMEM((rows, columns * wide), jnp.float32)],
    )
    return pl.pallas_call(
        functools.partial(out_kernel, blocks, columns, len(gated)),
        grid_spec=spec,
        out_shape=jax.ShapeDtypeStruct((rows, columns * wide), kind),
        compiler_params=pltpu.CompilerParams(vmem_limit_bytes=VMEM),
        cost_estimate=LIGHT,
        name="out_project",
    )(order, *gated, *[block for found in weights for block in found], *held)


def normalised(x, gain):
    values = x.astype(jnp.float32)
    squares = jnp.mean(values * values, axis=1, keepdims=True)
    return (values * lax.rsqrt(squares + 1e-06) * gain).astype(jnp.bfloat16)


def per_device(x_rows, norm_gain, in_weight, feat_filter, inner_filter, out_weight):
    tokens, model = x_rows.shape
    depth, _, chans_here = in_weight.shape
    seqs, chans = lax.axis_size("seq"), lax.axis_size("chan")
    near = 2 if seqs % 2 == 0 else 1
    far = seqs // near
    seq, chan = lax.axis_index("seq"), lax.axis_index("chan")
    e, g = seq // near, seq % near
    feat, filt = feat_filter.shape[0], inner_filter.shape[0]

    def from_near(block, k):
        pairs = [(a * near + (b + k) % near, a * near + b) for a in range(far) for b in range(near)]
        return lax.ppermute(block, "seq", pairs)

    def from_far(block, k):
        pairs = [((a + k) % far * near + b, a * near + b) for a in range(far) for b in range(near)]
        return lax.ppermute(block, "seq", pairs)

    def columns_of(rows, group):
        return jnp.concatenate(
            [
                lax.dynamic_slice_in_dim(rows, (group * near + (g + i) % near) * depth, depth, 1)
                for i in range(near)
            ],
            axis=1,
        )

    together = lax.optimization_barrier
    units = chans_here // LANES
    edges = [LANES * (units * part // 8) for part in EIGHTHS]
    cuts = [slice(a, b) for a, b in zip(edges, edges[1:])]
    first = in_weight[:, :, cuts[0]].transpose(1, 0, 2)
    in_weight, first = together((in_weight, first))
    owns = [first] + [in_weight[:, :, cut].transpose(1, 0, 2) for cut in cuts[1:]]
    weights = [[own] + [from_near(own, k) for k in range(1, near)] for own in owns]
    width = out_weight.shape[1] // OUT_CHUNKS
    rows = [out_weight[:, m * width : (m + 1) * width] for m in range(OUT_CHUNKS)]

    near_rows = [[from_near(block, k) for k in range(1, near)] for block in rows]

    share = tokens // chans
    before = lax.ppermute(
        x_rows[tokens - HALO :], "seq", [(a, a + 1) for a in range(seqs - 1)]
    )
    part = normalised(lax.dynamic_slice_in_dim(x_rows, chan * share, share, 0), norm_gain)
    pieces = [
        from_far(columns_of(part, (e - k) % far), k) for k in range(1, far)
    ]
    pieces, before, rows, owns, near_rows[0] = together(
        (pieces, before, rows, owns, near_rows[0])
    )
    theirs = [lax.all_gather(piece, "chan", axis=0, tiled=True) for piece in pieces]
    before = normalised(before, norm_gain)
    theirs_before = [from_far(columns_of(before, (e - k) % far), k) for k in range(1, far)]
    mine = columns_of(normalised(x_rows, norm_gain), e)
    mine_before = columns_of(before, e)
    taps = jnp.concatenate([feat_filter.reshape(feat * 3, chans_here), inner_filter], axis=0)

    across = [[from_far(block, a) for a in range(1, far)] for block in rows]
    theirs, theirs_before, weights[0], mine, mine_before, across = together(
        (theirs, theirs_before, weights[0], mine, mine_before, across)
    )

    gated, done = [], []
    for j in range(CHUNKS):
        sums = [
            from_far(project(theirs[k], theirs_before[k], weights[j], after=done), far - 1 - k)
            for k in range(far - 1)
        ]
        projected = project(mine, mine_before, weights[j], sums)
        if j == 0:
            projected, weights[1], near_rows[1] = together((projected, weights[1], near_rows[1]))
            beyond = [
                [from_far(block, a) for a in range(1, far) for block in found] for found in near_rows[:2]
            ]
        elif j < CHUNKS - 1:
            turn = min(j - 1, 1)
            projected, weights[j + 1], beyond[turn] = together(
                (projected, weights[j + 1], beyond[turn])
            )
        else:
            projected, near_rows[2:] = together((projected, near_rows[2:]))
            beyond += [
                [from_far(block, a) for a in range(1, far) for block in found] for found in near_rows[2:]
            ]
        mixed, mark = short_mix(projected, taps[:, cuts[j]], feat, filt)
        done = [mark]
        if j > 0:
            mixed, gated[j - 1] = together((mixed, gated[j - 1]))
        gated.append(lax.all_gather(mixed, "chan", axis=0))

    order = jnp.stack(
        [(e + a) % far * near + (g + b) % near for a in range(far) for b in range(near)]
    ).astype(jnp.int32)
    blocks = []
    for m in range(OUT_CHUNKS):
        found = [rows[m]] + near_rows[m]
        for a in range(1, far):
            found += [across[m][a - 1]] + beyond[m][(a - 1) * (near - 1) : a * (near - 1)]
        blocks.append([block.reshape(-1, chans_here, block.shape[1]) for block in found])
    half = OUT_CHUNKS // 2
    first = out_project(order, gated[:-1], 0, blocks[:half], jnp.float32)
    first, blocks[half:] = together((first, blocks[half:]))
    second = out_project(order, gated[:-1], 0, blocks[half:], jnp.float32)
    first, second, last = together((first, second, gated[-1]))
    out = out_project(order, [last], edges[CHUNKS - 1], blocks, jnp.bfloat16, [first, second])
    got = lax.all_to_all(
        out.reshape(chans, share, -1), "chan", split_axis=0, concat_axis=0, tiled=True
    )
    return got.transpose(1, 0, 2).reshape(share, -1)


def solution(mesh):
    return jax.shard_map(
        per_device,
        mesh=mesh,
        in_specs=(
            P("seq", None),
            P(),
            P("seq", None, "chan"),
            P(None, None, "chan"),
            P(None, "chan"),
            P("seq", "chan"),
        ),
        out_specs=P(("seq", "chan"), None),
        check_vma=False,
    )
```

```python
import functools

import jax
import jax.numpy as jnp
from jax import lax
from jax.experimental import pallas as pl
from jax.experimental.pallas import tpu as pltpu
from jax.sharding import PartitionSpec as P

HALO = 16
LANES = 128
EIGHTHS = (0, 2, 4, 6, 8)
CHUNKS = len(EIGHTHS) - 1
OUT_CHUNKS = 4
VMEM = 40 * 2**20
MARK = pl.BlockSpec((8, 128), lambda i: (0, 0))
MARK_SHAPE = jax.ShapeDtypeStruct((8, 128), jnp.float32)
LIGHT = pl.CostEstimate(flops=1024, bytes_accessed=1024, transcendentals=0)


def project_kernel(count, extra, tail, *refs):
    x_ref, refs = refs[0], refs[1:]
    halo_ref = refs[0] if tail else None
    weights = refs[tail : tail + count]
    received = refs[tail + count : tail + count + extra]
    received_tail = refs[tail + count + extra : tail + count + extra * (1 + tail)]
    out_ref, mark_ref = refs[-2:]
    parts, depth, width = weights[0].shape
    tile = x_ref.shape[0]
    step = pl.program_id(0)

    def products(ref, sums, start, size):
        for part in range(parts):
            cut = slice(part * width, (part + 1) * width)
            total = jnp.dot(ref[:, :depth], weights[0][part], preferred_element_type=jnp.float32)
            for i in range(1, count):
                total += jnp.dot(
                    ref[:, i * depth : (i + 1) * depth],
                    weights[i][part],
                    preferred_element_type=jnp.float32,
                )
            for other in sums:
                total += other[:, cut].astype(jnp.float32)
            out_ref[pl.ds(start, size), cut] = total.astype(out_ref.dtype)

    products(x_ref, received, pl.multiple_of(step * tile, tile), tile)

    @pl.when(step == 0)
    def _():
        mark_ref[...] = jnp.zeros_like(mark_ref)
        if tail:
            size = halo_ref.shape[0]
            products(halo_ref, received_tail, out_ref.shape[0] - size, size)


def project(x, half, halo, weights, received=(), after=()):
    rows, depth = x.shape[0] // 2, x.shape[1]
    extra = HALO if halo else 0
    columns = weights[0].shape[0] * weights[0].shape[2]
    tile = min(rows, 256)
    steps = rows // tile
    whole = pl.BlockSpec(weights[0].shape, lambda i: (0, 0, 0), pipeline_mode=pl.Buffered(1))
    tails = [pl.BlockSpec((HALO, columns), lambda i: (rows // HALO, 0))] if halo else []
    return pl.pallas_call(
        functools.partial(project_kernel, len(weights), len(received), len(halo)),
        grid=(steps,),
        in_specs=[pl.BlockSpec((tile, depth), lambda i: (half * steps + i, 0))]
        + [pl.BlockSpec((HALO, depth), lambda i: (0, 0))] * len(halo)
        + [whole] * len(weights)
        + [pl.BlockSpec((tile, columns), lambda i: (i, 0))] * len(received)
        + tails * len(received)
        + [pl.BlockSpec(memory_space=pl.ANY)] * len(after),
        out_specs=[pl.BlockSpec((rows + extra, columns), lambda i: (0, 0)), MARK],
        out_shape=[jax.ShapeDtypeStruct((rows + extra, columns), jnp.bfloat16), MARK_SHAPE],
        compiler_params=pltpu.CompilerParams(vmem_limit_bytes=VMEM),
        cost_estimate=LIGHT,
        name="project",
    )(x, *halo, *weights, *received, *(received if halo else ()), *after)


def mix_kernel(feat, filt, qh, kh, vh, qa, ka, va, qb, kb, vb, taps, out_ref, mark_ref, ext, prod):
    half = qa.shape[0]
    rows = 2 * half
    mark_ref[...] = jnp.zeros_like(mark_ref)
    for i, (h, a, b) in enumerate(((qh, qa, qb), (kh, ka, kb), (vh, va, vb))):
        ext[i, :HALO, :] = h[...].astype(jnp.float32)
        ext[i, HALO : HALO + half, :] = a[...].astype(jnp.float32)
        ext[i, HALO + half :, :] = b[...].astype(jnp.float32)
    tile = min(rows, 128)

    def featured(i, start, size):
        total = taps[i : i + 1, :] * ext[i, pl.ds(start, size), :]
        for j in range(1, feat):
            total += taps[3 * j + i : 3 * j + i + 1, :] * ext[i, pl.ds(start - j, size), :]
        return total

    for t in range(rows // tile):
        base = HALO + t * tile
        prod[...] = featured(1, base - 8, tile + 8) * featured(2, base - 8, tile + 8)
        total = taps[3 * feat : 3 * feat + 1, :] * prod[pl.ds(8, tile), :]
        for j in range(1, filt):
            total += taps[3 * feat + j : 3 * feat + j + 1, :] * prod[pl.ds(8 - j, tile), :]
        out_ref[t * tile : (t + 1) * tile, :] = (featured(0, base, tile) * total).astype(out_ref.dtype)


def short_mix(projected, taps, feat, filt):
    half, width = projected[1].shape[0], projected[1].shape[1] // 3
    rows = 2 * half
    lanes = LANES
    steps = width // lanes

    def part(i, size, row):
        return pl.BlockSpec((size, lanes), lambda b: (row, i * steps + b))

    tile = min(rows, 128)
    return pl.pallas_call(
        functools.partial(mix_kernel, feat, filt),
        grid=(steps,),
        in_specs=[part(i, HALO, half // HALO) for i in range(3)]
        + [part(i, half, 0) for i in range(3)] * 2
        + [pl.BlockSpec((taps.shape[0], lanes), lambda b: (0, b))],
        out_specs=[pl.BlockSpec((rows, lanes), lambda b: (0, b)), MARK],
        out_shape=[jax.ShapeDtypeStruct((rows, width), jnp.bfloat16), MARK_SHAPE],
        scratch_shapes=[
            pltpu.VMEM((3, HALO + rows, lanes), jnp.float32),
            pltpu.VMEM((tile + 8, lanes), jnp.float32),
        ],
        compiler_params=pltpu.CompilerParams(vmem_limit_bytes=VMEM),
        cost_estimate=LIGHT,
        name="short_mix",
    )(*projected[:1] * 6, *projected[1:] * 3, taps)


def out_kernel(blocks, columns, count, order, *refs):
    gated = refs[:count]
    weights = refs[count : count + columns * blocks]
    held, out_ref = refs[count + columns * blocks : -1], refs[-1]
    per_block, _, wide = weights[0].shape
    for m in range(columns):
        if held:
            each = columns // len(held)
            total = held[m // each][:, m % each * wide : (m % each + 1) * wide]
        else:
            total = jnp.zeros((out_ref.shape[0], wide), jnp.float32)
        for b in range(blocks):
            for i in range(per_block):
                row = 0
                for ref in gated:
                    size = ref.shape[2]
                    total += jnp.dot(
                        ref[order[b] * per_block + i],
                        weights[m * blocks + b][i, row : row + size, :],
                        preferred_element_type=jnp.float32,
                    )
                    row += size
        out_ref[:, m * wide : (m + 1) * wide] = total.astype(out_ref.dtype)


def out_project(order, gated, start, weights, kind, held=()):
    chans, rows, _ = gated[0].shape
    size = sum(block.shape[2] for block in gated)
    per_block, _, wide = weights[0][0].shape
    columns, blocks = len(weights), len(weights[0])
    tile = min(rows, 256)
    piece = pl.BlockSpec(
        (per_block, size, wide), lambda i, o: (0, start // size, 0), pipeline_mode=pl.Buffered(1)
    )
    spec = pltpu.PrefetchScalarGridSpec(
        num_scalar_prefetch=1,
        grid=(rows // tile,),
        in_specs=[
            pl.BlockSpec((chans, tile, block.shape[2]), lambda i, o: (0, i, 0)) for block in gated
        ]
        + [piece] * (columns * blocks)
        + [pl.BlockSpec((tile, block.shape[1]), lambda i, o: (i, 0)) for block in held],
        out_specs=pl.BlockSpec((tile, columns * wide), lambda i, o: (i, 0)),
    )
    return pl.pallas_call(
        functools.partial(out_kernel, blocks, columns, len(gated)),
        grid_spec=spec,
        out_shape=jax.ShapeDtypeStruct((rows, columns * wide), kind),
        compiler_params=pltpu.CompilerParams(vmem_limit_bytes=VMEM),
        cost_estimate=LIGHT,
        name="out_project",
    )(order, *gated, *[block for found in weights for block in found], *held)


def normalised(x, gain):
    values = x.astype(jnp.float32)
    squares = jnp.mean(values * values, axis=1, keepdims=True)
    return (values * lax.rsqrt(squares + 1e-06) * gain).astype(jnp.bfloat16)


def per_device(x_rows, norm_gain, in_weight, feat_filter, inner_filter, out_weight):
    tokens, model = x_rows.shape
    depth, _, chans_here = in_weight.shape
    seqs, chans = lax.axis_size("seq"), lax.axis_size("chan")
    near = 2 if seqs % 2 == 0 else 1
    far = seqs // near
    seq, chan = lax.axis_index("seq"), lax.axis_index("chan")
    e, g = seq // near, seq % near
    feat, filt = feat_filter.shape[0], inner_filter.shape[0]

    def from_near(block, k):
        pairs = [(a * near + (b + k) % near, a * near + b) for a in range(far) for b in range(near)]
        return lax.ppermute(block, "seq", pairs)

    def from_far(block, k):
        pairs = [((a + k) % far * near + b, a * near + b) for a in range(far) for b in range(near)]
        return lax.ppermute(block, "seq", pairs)

    def columns_of(rows, group):
        return jnp.concatenate(
            [
                lax.dynamic_slice_in_dim(rows, (group * near + (g + i) % near) * depth, depth, 1)
                for i in range(near)
            ],
            axis=1,
        )

    together = lax.optimization_barrier
    units = chans_here // LANES
    edges = [LANES * (units * part // 8) for part in EIGHTHS]
    cuts = [slice(a, b) for a, b in zip(edges, edges[1:])]
    first = in_weight[:, :, cuts[0]].transpose(1, 0, 2)
    in_weight, first = together((in_weight, first))
    owns = [first] + [in_weight[:, :, cut].transpose(1, 0, 2) for cut in cuts[1:]]
    weights = [[own] + [from_near(own, k) for k in range(1, near)] for own in owns]
    width = out_weight.shape[1] // OUT_CHUNKS
    rows = [out_weight[:, m * width : (m + 1) * width] for m in range(OUT_CHUNKS)]

    near_rows = [[from_near(block, k) for k in range(1, near)] for block in rows]

    share = tokens // chans
    before = lax.ppermute(
        x_rows[tokens - HALO :], "seq", [(a, a + 1) for a in range(seqs - 1)]
    )
    part = normalised(lax.dynamic_slice_in_dim(x_rows, chan * share, share, 0), norm_gain)
    pieces = [
        from_far(columns_of(part, (e - k) % far), k) for k in range(1, far)
    ]
    pieces, before, rows, owns, near_rows[0] = together(
        (pieces, before, rows, owns, near_rows[0])
    )
    theirs = [lax.all_gather(piece, "chan", axis=0, tiled=True) for piece in pieces]
    before = normalised(before, norm_gain)
    theirs_before = [from_far(columns_of(before, (e - k) % far), k) for k in range(1, far)]
    taps = jnp.concatenate([feat_filter.reshape(feat * 3, chans_here), inner_filter], axis=0)
    across = [[from_far(block, a) for a in range(1, far)] for block in rows]
    x_rows, across[0] = together((x_rows, across[0]))
    normed, across[1] = together((normalised(x_rows, norm_gain), across[1]))
    mine = columns_of(normed, e)
    mine_before = columns_of(before, e)
    theirs, theirs_before, weights[0], mine, mine_before, across = together(
        (theirs, theirs_before, weights[0], mine, mine_before, across)
    )

    def beyond(m):
        return [[from_far(block, a) for block in near_rows[m]] for a in range(1, far)]

    gated, done, diagonal = [], [], []
    for j in range(CHUNKS):
        sums, after = [], list(done)
        for half in (0, 1):
            made = [
                project(theirs[k], half, [] if half else [theirs_before[k]], weights[j], after=after)
                for k in range(far - 1)
            ]
            after = [mark for _, mark in made]
            sums.append([from_far(made[k][0], far - 1 - k) for k in range(far - 1)])
        first, mark = project(mine, 0, [mine_before], weights[j], sums[0])
        second, _ = project(mine, 1, [], weights[j], sums[1], after=[mark])
        projected = [first, second]
        if j == 0:
            projected, weights[1], near_rows[1] = together((projected, weights[1], near_rows[1]))
        elif j < CHUNKS - 1:
            diagonal.append(beyond(j - 1))
            projected, weights[j + 1], diagonal[-1] = together(
                (projected, weights[j + 1], diagonal[-1])
            )
        else:
            projected, near_rows[2:] = together((projected, near_rows[2:]))
            diagonal += [beyond(2), beyond(3)]
        mixed, mark = short_mix(projected, taps[:, cuts[j]], feat, filt)
        done = [mark]
        if j > 0:
            mixed, gated[j - 1] = together((mixed, gated[j - 1]))
        gated.append(lax.all_gather(mixed, "chan", axis=0))

    order = jnp.stack(
        [(e + a) % far * near + (g + b) % near for a in range(far) for b in range(near)]
    ).astype(jnp.int32)
    blocks = []
    for m in range(OUT_CHUNKS):
        found = [rows[m]] + near_rows[m]
        for a in range(1, far):
            found += [across[m][a - 1]] + diagonal[m][a - 1]
        blocks.append([block.reshape(-1, chans_here, block.shape[1]) for block in found])
    half = OUT_CHUNKS // 2
    first = out_project(order, gated[:-1], 0, blocks[:half], jnp.float32)
    first, blocks[half:] = together((first, blocks[half:]))
    second = out_project(order, gated[:-1], 0, blocks[half:], jnp.float32)
    first, second, last = together((first, second, gated[-1]))
    out = out_project(order, [last], edges[CHUNKS - 1], blocks, jnp.bfloat16, [first, second])
    got = lax.all_to_all(
        out.reshape(chans, share, -1), "chan", split_axis=0, concat_axis=0, tiled=True
    )
    return got.transpose(1, 0, 2).reshape(share, -1)


def solution(mesh):
    return jax.shard_map(
        per_device,
        mesh=mesh,
        in_specs=(
            P("seq", None),
            P(),
            P("seq", None, "chan"),
            P(None, None, "chan"),
            P(None, "chan"),
            P("seq", "chan"),
        ),
        out_specs=P(("seq", "chan"), None),
        check_vma=False,
    )
```

```python
import functools

import jax
import jax.numpy as jnp
from jax import lax
from jax.experimental import pallas as pl
from jax.experimental.pallas import tpu as pltpu
from jax.sharding import PartitionSpec as P

HALO = 16
LANES = 128
EIGHTHS = (0, 2, 4, 6, 8)
CHUNKS = len(EIGHTHS) - 1
OUT_CHUNKS = 4
VMEM = 40 * 2**20
MARK = pl.BlockSpec((8, 128), lambda i: (0, 0))
MARK_SHAPE = jax.ShapeDtypeStruct((8, 128), jnp.float32)
LIGHT = pl.CostEstimate(flops=1024, bytes_accessed=1024, transcendentals=0)


def project_kernel(count, extra, tail, *refs):
    x_ref, refs = refs[0], refs[1:]
    halo_ref = refs[0] if tail else None
    weights = refs[tail : tail + count]
    received = refs[tail + count : tail + count + extra]
    received_tail = refs[tail + count + extra : tail + count + extra * (1 + tail)]
    out_ref, mark_ref = refs[-2:]
    parts, depth, width = weights[0].shape
    tile = x_ref.shape[0]
    step = pl.program_id(0)

    def products(ref, sums, start, size):
        for part in range(parts):
            cut = slice(part * width, (part + 1) * width)
            total = jnp.dot(ref[:, :depth], weights[0][part], preferred_element_type=jnp.float32)
            for i in range(1, count):
                total += jnp.dot(
                    ref[:, i * depth : (i + 1) * depth],
                    weights[i][part],
                    preferred_element_type=jnp.float32,
                )
            for other in sums:
                total += other[:, cut].astype(jnp.float32)
            out_ref[pl.ds(start, size), cut] = total.astype(out_ref.dtype)

    products(x_ref, received, pl.multiple_of(step * tile, tile), tile)

    @pl.when(step == 0)
    def _():
        mark_ref[...] = jnp.zeros_like(mark_ref)
        if tail:
            size = halo_ref.shape[0]
            products(halo_ref, received_tail, out_ref.shape[0] - size, size)


def project(x, half, halo, weights, received=(), after=()):
    rows, depth = x.shape[0] // 2, x.shape[1]
    extra = HALO if halo else 0
    columns = weights[0].shape[0] * weights[0].shape[2]
    tile = min(rows, 256)
    steps = rows // tile
    whole = pl.BlockSpec(weights[0].shape, lambda i: (0, 0, 0), pipeline_mode=pl.Buffered(1))
    tails = [pl.BlockSpec((HALO, columns), lambda i: (rows // HALO, 0))] if halo else []
    return pl.pallas_call(
        functools.partial(project_kernel, len(weights), len(received), len(halo)),
        grid=(steps,),
        in_specs=[pl.BlockSpec((tile, depth), lambda i: (half * steps + i, 0))]
        + [pl.BlockSpec((HALO, depth), lambda i: (0, 0))] * len(halo)
        + [whole] * len(weights)
        + [pl.BlockSpec((tile, columns), lambda i: (i, 0))] * len(received)
        + tails * len(received)
        + [pl.BlockSpec(memory_space=pl.ANY)] * len(after),
        out_specs=[pl.BlockSpec((rows + extra, columns), lambda i: (0, 0)), MARK],
        out_shape=[jax.ShapeDtypeStruct((rows + extra, columns), jnp.bfloat16), MARK_SHAPE],
        compiler_params=pltpu.CompilerParams(vmem_limit_bytes=VMEM),
        cost_estimate=LIGHT,
        name="project",
    )(x, *halo, *weights, *received, *(received if halo else ()), *after)


def mix_kernel(feat, filt, qh, kh, vh, qa, ka, va, qb, kb, vb, taps, out_ref, mark_ref, ext, prod):
    half = qa.shape[0]
    rows = 2 * half
    mark_ref[...] = jnp.zeros_like(mark_ref)
    for i, (h, a, b) in enumerate(((qh, qa, qb), (kh, ka, kb), (vh, va, vb))):
        ext[i, :HALO, :] = h[...].astype(jnp.float32)
        ext[i, HALO : HALO + half, :] = a[...].astype(jnp.float32)
        ext[i, HALO + half :, :] = b[...].astype(jnp.float32)
    tile = min(rows, 128)

    def featured(i, start, size):
        total = taps[i : i + 1, :] * ext[i, pl.ds(start, size), :]
        for j in range(1, feat):
            total += taps[3 * j + i : 3 * j + i + 1, :] * ext[i, pl.ds(start - j, size), :]
        return total

    for t in range(rows // tile):
        base = HALO + t * tile
        prod[...] = featured(1, base - 8, tile + 8) * featured(2, base - 8, tile + 8)
        total = taps[3 * feat : 3 * feat + 1, :] * prod[pl.ds(8, tile), :]
        for j in range(1, filt):
            total += taps[3 * feat + j : 3 * feat + j + 1, :] * prod[pl.ds(8 - j, tile), :]
        out_ref[t * tile : (t + 1) * tile, :] = (featured(0, base, tile) * total).astype(out_ref.dtype)


def short_mix(projected, taps, feat, filt):
    half, width = projected[1].shape[0], projected[1].shape[1] // 3
    rows = 2 * half
    lanes = LANES
    steps = width // lanes

    def part(i, size, row):
        return pl.BlockSpec((size, lanes), lambda b: (row, i * steps + b))

    tile = min(rows, 128)
    return pl.pallas_call(
        functools.partial(mix_kernel, feat, filt),
        grid=(steps,),
        in_specs=[part(i, HALO, half // HALO) for i in range(3)]
        + [part(i, half, 0) for i in range(3)] * 2
        + [pl.BlockSpec((taps.shape[0], lanes), lambda b: (0, b))],
        out_specs=[pl.BlockSpec((rows, lanes), lambda b: (0, b)), MARK],
        out_shape=[jax.ShapeDtypeStruct((rows, width), jnp.bfloat16), MARK_SHAPE],
        scratch_shapes=[
            pltpu.VMEM((3, HALO + rows, lanes), jnp.float32),
            pltpu.VMEM((tile + 8, lanes), jnp.float32),
        ],
        compiler_params=pltpu.CompilerParams(vmem_limit_bytes=VMEM),
        cost_estimate=LIGHT,
        name="short_mix",
    )(*projected[:1] * 6, *projected[1:] * 3, taps)


def out_kernel(blocks, columns, count, order, *refs):
    gated = refs[:count]
    weights = refs[count : count + columns * blocks]
    held, out_ref = refs[count + columns * blocks : -1], refs[-1]
    per_block, _, wide = weights[0].shape
    for m in range(columns):
        if held:
            place, at = 0, m * wide
            while at >= held[place].shape[1]:
                at -= held[place].shape[1]
                place += 1
            total = held[place][:, at : at + wide]
        else:
            total = jnp.zeros((out_ref.shape[0], wide), jnp.float32)
        for b in range(blocks):
            for i in range(per_block):
                row = 0
                for ref in gated:
                    size = ref.shape[2]
                    total += jnp.dot(
                        ref[order[b] * per_block + i],
                        weights[m * blocks + b][i, row : row + size, :],
                        preferred_element_type=jnp.float32,
                    )
                    row += size
        out_ref[:, m * wide : (m + 1) * wide] = total.astype(out_ref.dtype)


def out_project(order, gated, start, weights, kind, held=()):
    chans, rows, _ = gated[0].shape
    size = sum(block.shape[2] for block in gated)
    per_block, _, wide = weights[0][0].shape
    columns, blocks = len(weights), len(weights[0])
    tile = min(rows, 256)
    piece = pl.BlockSpec(
        (per_block, size, wide), lambda i, o: (0, start // size, 0), pipeline_mode=pl.Buffered(1)
    )
    spec = pltpu.PrefetchScalarGridSpec(
        num_scalar_prefetch=1,
        grid=(rows // tile,),
        in_specs=[
            pl.BlockSpec((chans, tile, block.shape[2]), lambda i, o: (0, i, 0)) for block in gated
        ]
        + [piece] * (columns * blocks)
        + [pl.BlockSpec((tile, block.shape[1]), lambda i, o: (i, 0)) for block in held],
        out_specs=pl.BlockSpec((tile, columns * wide), lambda i, o: (i, 0)),
    )
    return pl.pallas_call(
        functools.partial(out_kernel, blocks, columns, len(gated)),
        grid_spec=spec,
        out_shape=jax.ShapeDtypeStruct((rows, columns * wide), kind),
        compiler_params=pltpu.CompilerParams(vmem_limit_bytes=VMEM),
        cost_estimate=LIGHT,
        name="out_project",
    )(order, *gated, *[block for found in weights for block in found], *held)


def normalised(x, gain):
    values = x.astype(jnp.float32)
    squares = jnp.mean(values * values, axis=1, keepdims=True)
    return (values * lax.rsqrt(squares + 1e-06) * gain).astype(jnp.bfloat16)


def per_device(x_rows, norm_gain, in_weight, feat_filter, inner_filter, out_weight):
    tokens, model = x_rows.shape
    depth, _, chans_here = in_weight.shape
    seqs, chans = lax.axis_size("seq"), lax.axis_size("chan")
    near = 2 if seqs % 2 == 0 else 1
    far = seqs // near
    seq, chan = lax.axis_index("seq"), lax.axis_index("chan")
    e, g = seq // near, seq % near
    feat, filt = feat_filter.shape[0], inner_filter.shape[0]

    def from_near(block, k):
        pairs = [(a * near + (b + k) % near, a * near + b) for a in range(far) for b in range(near)]
        return lax.ppermute(block, "seq", pairs)

    def from_far(block, k):
        pairs = [((a + k) % far * near + b, a * near + b) for a in range(far) for b in range(near)]
        return lax.ppermute(block, "seq", pairs)

    def columns_of(rows, group):
        return jnp.concatenate(
            [
                lax.dynamic_slice_in_dim(rows, (group * near + (g + i) % near) * depth, depth, 1)
                for i in range(near)
            ],
            axis=1,
        )

    together = lax.optimization_barrier
    units = chans_here // LANES
    edges = [LANES * (units * part // 8) for part in EIGHTHS]
    cuts = [slice(a, b) for a, b in zip(edges, edges[1:])]
    first = in_weight[:, :, cuts[0]].transpose(1, 0, 2)
    in_weight, first = together((in_weight, first))
    owns = [first] + [in_weight[:, :, cut].transpose(1, 0, 2) for cut in cuts[1:]]
    weights = [[own] + [from_near(own, k) for k in range(1, near)] for own in owns]
    width = out_weight.shape[1] // OUT_CHUNKS
    rows = [out_weight[:, m * width : (m + 1) * width] for m in range(OUT_CHUNKS)]

    near_rows = [[from_near(block, k) for k in range(1, near)] for block in rows]

    share = tokens // chans
    before = lax.ppermute(
        x_rows[tokens - HALO :], "seq", [(a, a + 1) for a in range(seqs - 1)]
    )
    part = normalised(lax.dynamic_slice_in_dim(x_rows, chan * share, share, 0), norm_gain)
    pieces = [
        from_far(columns_of(part, (e - k) % far), k) for k in range(1, far)
    ]
    pieces, before, rows, owns, near_rows[0] = together(
        (pieces, before, rows, owns, near_rows[0])
    )
    theirs = [lax.all_gather(piece, "chan", axis=0, tiled=True) for piece in pieces]
    before = normalised(before, norm_gain)
    theirs_before = [from_far(columns_of(before, (e - k) % far), k) for k in range(1, far)]
    taps = jnp.concatenate([feat_filter.reshape(feat * 3, chans_here), inner_filter], axis=0)
    rows[1:], theirs_before = together((rows[1:], theirs_before))
    across = [[from_far(block, a) for a in range(1, far)] for block in rows]
    normed, across[0] = together((normalised(x_rows, norm_gain), across[0]))
    mine, across[1] = together((columns_of(normed, e), across[1]))
    mine_before = columns_of(before, e)
    theirs, theirs_before, weights[0], mine, mine_before, across[:3] = together(
        (theirs, theirs_before, weights[0], mine, mine_before, across[:3])
    )

    def beyond(m):
        return [[from_far(block, a) for block in near_rows[m]] for a in range(1, far)]

    def sideways(m):
        return [[from_near(block, k) for k in range(1, near)] for block in across[m]]

    gated, done, diagonal = [], [], []
    for j in range(CHUNKS):
        sums, after = [], list(done)
        for half in (0, 1):
            made = [
                project(theirs[k], half, [] if half else [theirs_before[k]], weights[j], after=after)
                for k in range(far - 1)
            ]
            after = [mark for _, mark in made]
            sums.append([from_far(made[k][0], far - 1 - k) for k in range(far - 1)])
        first, mark = project(mine, 0, [mine_before], weights[j], sums[0])
        second, _ = project(mine, 1, [], weights[j], sums[1], after=[mark])
        projected = [first, second]
        if j == 0:
            projected, weights[1], near_rows[1], across[3] = together(
                (projected, weights[1], near_rows[1], across[3])
            )
        elif j == 1:
            diagonal.append(beyond(0))
            projected, weights[2], diagonal[0] = together((projected, weights[2], diagonal[0]))
        elif j == 2:
            diagonal.append(beyond(1))
            projected, weights[3], diagonal[1] = together((projected, weights[3], diagonal[1]))
        else:
            projected, near_rows[2:] = together((projected, near_rows[2:]))
            diagonal += [beyond(2), sideways(3)]
        mixed, mark = short_mix(projected, taps[:, cuts[j]], feat, filt)
        done = [mark]
        if j > 0:
            mixed, gated[j - 1] = together((mixed, gated[j - 1]))
        gated.append(lax.all_gather(mixed, "chan", axis=0))

    order = jnp.stack(
        [(e + a) % far * near + (g + b) % near for a in range(far) for b in range(near)]
    ).astype(jnp.int32)
    blocks = []
    for m in range(OUT_CHUNKS):
        found = [rows[m]] + near_rows[m]
        for a in range(1, far):
            found += [across[m][a - 1]] + diagonal[m][a - 1]
        blocks.append([block.reshape(-1, chans_here, block.shape[1]) for block in found])
    groups, partial = (blocks[:2], blocks[2:]), []
    for found in groups:
        if partial:
            partial[-1], found = together((partial[-1], found))
        partial.append(out_project(order, gated[:-1], 0, found, jnp.float32))
    partial, last = together((partial, gated[-1]))
    out = out_project(order, [last], edges[CHUNKS - 1], blocks, jnp.bfloat16, partial)
    got = lax.all_to_all(
        out.reshape(chans, share, -1), "chan", split_axis=0, concat_axis=0, tiled=True
    )
    return got.transpose(1, 0, 2).reshape(share, -1)


def solution(mesh):
    return jax.shard_map(
        per_device,
        mesh=mesh,
        in_specs=(
            P("seq", None),
            P(),
            P("seq", None, "chan"),
            P(None, None, "chan"),
            P(None, "chan"),
            P("seq", "chan"),
        ),
        out_specs=P(("seq", "chan"), None),
        check_vma=False,
    )
```

```python
import functools

import jax
import jax.numpy as jnp
from jax import lax
from jax.experimental import pallas as pl
from jax.experimental.pallas import tpu as pltpu
from jax.sharding import PartitionSpec as P

HALO = 16
LANES = 128
EIGHTHS = (0, 2, 4, 6, 8)
CHUNKS = len(EIGHTHS) - 1
OUT_CHUNKS = 4
VMEM = 40 * 2**20
MARK = pl.BlockSpec((8, 128), lambda i: (0, 0))
MARK_SHAPE = jax.ShapeDtypeStruct((8, 128), jnp.float32)
LIGHT = pl.CostEstimate(flops=1024, bytes_accessed=1024, transcendentals=0)


def project_kernel(count, extra, tail, *refs):
    x_ref, refs = refs[0], refs[1:]
    halo_ref = refs[0] if tail else None
    weights = refs[tail : tail + count]
    received = refs[tail + count : tail + count + extra]
    received_tail = refs[tail + count + extra : tail + count + extra * (1 + tail)]
    out_ref, mark_ref = refs[-2:]
    parts, depth, width = weights[0].shape
    tile = x_ref.shape[0]
    step = pl.program_id(0)

    def products(ref, sums, start, size):
        for part in range(parts):
            cut = slice(part * width, (part + 1) * width)
            total = jnp.dot(ref[:, :depth], weights[0][part], preferred_element_type=jnp.float32)
            for i in range(1, count):
                total += jnp.dot(
                    ref[:, i * depth : (i + 1) * depth],
                    weights[i][part],
                    preferred_element_type=jnp.float32,
                )
            for other in sums:
                total += other[:, cut].astype(jnp.float32)
            out_ref[pl.ds(start, size), cut] = total.astype(out_ref.dtype)

    products(x_ref, received, pl.multiple_of(step * tile, tile), tile)

    @pl.when(step == 0)
    def _():
        mark_ref[...] = jnp.zeros_like(mark_ref)
        if tail:
            size = halo_ref.shape[0]
            products(halo_ref, received_tail, out_ref.shape[0] - size, size)


def project(x, half, halo, weights, received=(), after=()):
    rows, depth = x.shape[0] // 2, x.shape[1]
    extra = HALO if halo else 0
    columns = weights[0].shape[0] * weights[0].shape[2]
    tile = min(rows, 256)
    steps = rows // tile
    whole = pl.BlockSpec(weights[0].shape, lambda i: (0, 0, 0), pipeline_mode=pl.Buffered(1))
    tails = [pl.BlockSpec((HALO, columns), lambda i: (rows // HALO, 0))] if halo else []
    return pl.pallas_call(
        functools.partial(project_kernel, len(weights), len(received), len(halo)),
        grid=(steps,),
        in_specs=[pl.BlockSpec((tile, depth), lambda i: (half * steps + i, 0))]
        + [pl.BlockSpec((HALO, depth), lambda i: (0, 0))] * len(halo)
        + [whole] * len(weights)
        + [pl.BlockSpec((tile, columns), lambda i: (i, 0))] * len(received)
        + tails * len(received)
        + [pl.BlockSpec(memory_space=pl.ANY)] * len(after),
        out_specs=[pl.BlockSpec((rows + extra, columns), lambda i: (0, 0)), MARK],
        out_shape=[jax.ShapeDtypeStruct((rows + extra, columns), jnp.bfloat16), MARK_SHAPE],
        compiler_params=pltpu.CompilerParams(vmem_limit_bytes=VMEM),
        cost_estimate=LIGHT,
        name="project",
    )(x, *halo, *weights, *received, *(received if halo else ()), *after)


def mix_kernel(feat, filt, qh, kh, vh, qa, ka, va, qb, kb, vb, taps, out_ref, mark_ref, ext, prod):
    half = qa.shape[0]
    rows = 2 * half
    mark_ref[...] = jnp.zeros_like(mark_ref)
    for i, (h, a, b) in enumerate(((qh, qa, qb), (kh, ka, kb), (vh, va, vb))):
        ext[i, :HALO, :] = h[...].astype(jnp.float32)
        ext[i, HALO : HALO + half, :] = a[...].astype(jnp.float32)
        ext[i, HALO + half :, :] = b[...].astype(jnp.float32)
    tile = min(rows, 128)

    def featured(i, start, size):
        total = taps[i : i + 1, :] * ext[i, pl.ds(start, size), :]
        for j in range(1, feat):
            total += taps[3 * j + i : 3 * j + i + 1, :] * ext[i, pl.ds(start - j, size), :]
        return total

    for t in range(rows // tile):
        base = HALO + t * tile
        prod[...] = featured(1, base - 8, tile + 8) * featured(2, base - 8, tile + 8)
        total = taps[3 * feat : 3 * feat + 1, :] * prod[pl.ds(8, tile), :]
        for j in range(1, filt):
            total += taps[3 * feat + j : 3 * feat + j + 1, :] * prod[pl.ds(8 - j, tile), :]
        out_ref[t * tile : (t + 1) * tile, :] = (featured(0, base, tile) * total).astype(out_ref.dtype)


def short_mix(projected, taps, feat, filt):
    half, width = projected[1].shape[0], projected[1].shape[1] // 3
    rows = 2 * half
    lanes = LANES
    steps = width // lanes

    def part(i, size, row):
        return pl.BlockSpec((size, lanes), lambda b: (row, i * steps + b))

    tile = min(rows, 128)
    return pl.pallas_call(
        functools.partial(mix_kernel, feat, filt),
        grid=(steps,),
        in_specs=[part(i, HALO, half // HALO) for i in range(3)]
        + [part(i, half, 0) for i in range(3)] * 2
        + [pl.BlockSpec((taps.shape[0], lanes), lambda b: (0, b))],
        out_specs=[pl.BlockSpec((rows, lanes), lambda b: (0, b)), MARK],
        out_shape=[jax.ShapeDtypeStruct((rows, width), jnp.bfloat16), MARK_SHAPE],
        scratch_shapes=[
            pltpu.VMEM((3, HALO + rows, lanes), jnp.float32),
            pltpu.VMEM((tile + 8, lanes), jnp.float32),
        ],
        compiler_params=pltpu.CompilerParams(vmem_limit_bytes=VMEM),
        cost_estimate=LIGHT,
        name="short_mix",
    )(*projected[:1] * 6, *projected[1:] * 3, taps)


def out_kernel(blocks, columns, count, order, *refs):
    gated = refs[:count]
    weights = refs[count : count + columns * blocks]
    held, out_ref = refs[count + columns * blocks : -1], refs[-1]
    per_block, _, wide = weights[0].shape
    for m in range(columns):
        if held:
            place, at = 0, m * wide
            while at >= held[place].shape[1]:
                at -= held[place].shape[1]
                place += 1
            total = held[place][:, at : at + wide]
        else:
            total = jnp.zeros((out_ref.shape[0], wide), jnp.float32)
        for b in range(blocks):
            for i in range(per_block):
                row = 0
                for ref in gated:
                    size = ref.shape[2]
                    total += jnp.dot(
                        ref[order[b] * per_block + i],
                        weights[m * blocks + b][i, row : row + size, :],
                        preferred_element_type=jnp.float32,
                    )
                    row += size
        out_ref[:, m * wide : (m + 1) * wide] = total.astype(out_ref.dtype)


def out_project(order, gated, start, weights, kind, held=()):
    chans, rows, _ = gated[0].shape
    size = sum(block.shape[2] for block in gated)
    per_block, _, wide = weights[0][0].shape
    columns, blocks = len(weights), len(weights[0])
    tile = min(rows, 256)
    piece = pl.BlockSpec(
        (per_block, size, wide), lambda i, o: (0, start // size, 0), pipeline_mode=pl.Buffered(1)
    )
    spec = pltpu.PrefetchScalarGridSpec(
        num_scalar_prefetch=1,
        grid=(rows // tile,),
        in_specs=[
            pl.BlockSpec((chans, tile, block.shape[2]), lambda i, o: (0, i, 0)) for block in gated
        ]
        + [piece] * (columns * blocks)
        + [pl.BlockSpec((tile, block.shape[1]), lambda i, o: (i, 0)) for block in held],
        out_specs=pl.BlockSpec((tile, columns * wide), lambda i, o: (i, 0)),
    )
    return pl.pallas_call(
        functools.partial(out_kernel, blocks, columns, len(gated)),
        grid_spec=spec,
        out_shape=jax.ShapeDtypeStruct((rows, columns * wide), kind),
        compiler_params=pltpu.CompilerParams(vmem_limit_bytes=VMEM),
        cost_estimate=LIGHT,
        name="out_project",
    )(order, *gated, *[block for found in weights for block in found], *held)


def normalised(x, gain):
    values = x.astype(jnp.float32)
    squares = jnp.mean(values * values, axis=1, keepdims=True)
    return (values * lax.rsqrt(squares + 1e-06) * gain).astype(jnp.bfloat16)


def per_device(x_rows, norm_gain, in_weight, feat_filter, inner_filter, out_weight):
    tokens, model = x_rows.shape
    depth, _, chans_here = in_weight.shape
    seqs, chans = lax.axis_size("seq"), lax.axis_size("chan")
    near = 2 if seqs % 2 == 0 else 1
    far = seqs // near
    seq, chan = lax.axis_index("seq"), lax.axis_index("chan")
    e, g = seq // near, seq % near
    feat, filt = feat_filter.shape[0], inner_filter.shape[0]

    def from_near(block, k):
        pairs = [(a * near + (b + k) % near, a * near + b) for a in range(far) for b in range(near)]
        return lax.ppermute(block, "seq", pairs)

    def from_far(block, k):
        pairs = [((a + k) % far * near + b, a * near + b) for a in range(far) for b in range(near)]
        return lax.ppermute(block, "seq", pairs)

    def columns_of(rows, group):
        return jnp.concatenate(
            [
                lax.dynamic_slice_in_dim(rows, (group * near + (g + i) % near) * depth, depth, 1)
                for i in range(near)
            ],
            axis=1,
        )

    together = lax.optimization_barrier
    units = chans_here // LANES
    edges = [LANES * (units * part // 8) for part in EIGHTHS]
    cuts = [slice(a, b) for a, b in zip(edges, edges[1:])]
    first = in_weight[:, :, cuts[0]].transpose(1, 0, 2)
    in_weight, first = together((in_weight, first))
    owns = [first] + [in_weight[:, :, cut].transpose(1, 0, 2) for cut in cuts[1:]]
    weights = [[own] + [from_near(own, k) for k in range(1, near)] for own in owns]
    width = out_weight.shape[1] // OUT_CHUNKS
    rows = [out_weight[:, m * width : (m + 1) * width] for m in range(OUT_CHUNKS)]

    near_rows = [[from_near(block, k) for k in range(1, near)] for block in rows]

    share = tokens // chans
    before = lax.ppermute(
        x_rows[tokens - HALO :], "seq", [(a, a + 1) for a in range(seqs - 1)]
    )
    part = normalised(lax.dynamic_slice_in_dim(x_rows, chan * share, share, 0), norm_gain)
    pieces = [
        from_far(columns_of(part, (e - k) % far), k) for k in range(1, far)
    ]
    pieces, before, rows, owns, near_rows[0] = together(
        (pieces, before, rows, owns, near_rows[0])
    )
    theirs = [lax.all_gather(piece, "chan", axis=0, tiled=True) for piece in pieces]
    before = normalised(before, norm_gain)
    theirs_before = [from_far(columns_of(before, (e - k) % far), k) for k in range(1, far)]
    taps = jnp.concatenate([feat_filter.reshape(feat * 3, chans_here), inner_filter], axis=0)
    rows[1:], theirs_before = together((rows[1:], theirs_before))
    x_rows, theirs_before = together((x_rows, theirs_before))
    across = [[from_far(block, a) for a in range(1, far)] for block in rows]
    normed, across[0] = together((normalised(x_rows, norm_gain), across[0]))
    mine, across[1] = together((columns_of(normed, e), across[1]))
    mine_before = columns_of(before, e)
    theirs, theirs_before, weights[0], mine, mine_before, across[:3] = together(
        (theirs, theirs_before, weights[0], mine, mine_before, across[:3])
    )

    def beyond(m):
        return [[from_far(block, a) for block in near_rows[m]] for a in range(1, far)]

    def sideways(m):
        return [[from_near(block, k) for k in range(1, near)] for block in across[m]]

    gated, done, diagonal = [], [], []
    for j in range(CHUNKS):
        sums, after = [], list(done)
        for half in (0, 1):
            made = [
                project(theirs[k], half, [] if half else [theirs_before[k]], weights[j], after=after)
                for k in range(far - 1)
            ]
            after = [mark for _, mark in made]
            sums.append([from_far(made[k][0], far - 1 - k) for k in range(far - 1)])
        first, mark = project(mine, 0, [mine_before], weights[j], sums[0])
        second, _ = project(mine, 1, [], weights[j], sums[1], after=[mark])
        projected = [first, second]
        if j == 0:
            projected, weights[1], across[3] = together((projected, weights[1], across[3]))
        elif j == 1:
            diagonal.append(beyond(0))
            projected, weights[2], diagonal[0] = together((projected, weights[2], diagonal[0]))
        elif j == 2:
            projected, weights[3] = together((projected, weights[3]))
        else:
            projected, near_rows[1:3] = together((projected, near_rows[1:3]))
            diagonal += [beyond(1), beyond(2), sideways(3)]
        mixed, mark = short_mix(projected, taps[:, cuts[j]], feat, filt)
        done = [mark]
        if j > 0:
            mixed, gated[j - 1] = together((mixed, gated[j - 1]))
        gated.append(lax.all_gather(mixed, "chan", axis=0))

    order = jnp.stack(
        [(e + a) % far * near + (g + b) % near for a in range(far) for b in range(near)]
    ).astype(jnp.int32)
    blocks = []
    for m in range(OUT_CHUNKS):
        found = [rows[m]] + near_rows[m]
        for a in range(1, far):
            found += [across[m][a - 1]] + diagonal[m][a - 1]
        blocks.append([block.reshape(-1, chans_here, block.shape[1]) for block in found])
    groups, partial = (blocks[:1], blocks[1:2], blocks[2:]), []
    for found in groups:
        if partial:
            partial[-1], found = together((partial[-1], found))
        partial.append(out_project(order, gated[:-1], 0, found, jnp.float32))
    partial, last = together((partial, gated[-1]))
    out = out_project(order, [last], edges[CHUNKS - 1], blocks, jnp.bfloat16, partial)
    got = lax.all_to_all(
        out.reshape(chans, share, -1), "chan", split_axis=0, concat_axis=0, tiled=True
    )
    return got.transpose(1, 0, 2).reshape(share, -1)


def solution(mesh):
    return jax.shard_map(
        per_device,
        mesh=mesh,
        in_specs=(
            P("seq", None),
            P(),
            P("seq", None, "chan"),
            P(None, None, "chan"),
            P(None, "chan"),
            P("seq", "chan"),
        ),
        out_specs=P(("seq", "chan"), None),
        check_vma=False,
    )
```
